512 devices in a mesh: group: 8 (over y, core), member: 64 (over x, z).
Axes of the slice: x: 4, y: 4, z: 16, core: 2. Of those that a mesh axis runs over, the one named last changes fastest.
Arguments:
- state: float32 [8192, 64, 128], P(('group', 'member')), may hold values from -2.5 to 2.5
- blocks: bfloat16 [8192, 6, 128, 128], P(('group', 'member')), may hold values from -1 to 1
- rate: float32 [8192, 128], P(('group', 'member')), may hold values from 0.1 to 1
- own_col: int32 [8192], P(('group', 'member')), may hold values from 0 to 15
- member_col: int32 [8192, 4], P(('group', 'member')), may hold values from 0 to 63, as said below
- group_col: int32 [8192, 1], P(('group', 'member')), may hold values from 0 to 15, as said below
- member_send: int32 [512, 64], P(('group', 'member')), may hold values from 0 to 15
- group_send: int32 [512, 16], P(('group', 'member')), may hold values from 0 to 15
Outputs:
- new_state: float32 [8192, 64, 128], P(('group', 'member'))
The draws below stay inside these ranges and needn't reach their ends.
Inputs may be any that keep to these rules, and one draw needn't show every extreme that they name: `member_col`: on each device the 64 entries of its rows name every member index equally often. `group_col`: on each device the 16 entries of its rows name every slot equally often.
All inputs are finite; a program needn't handle non-finite values.
Results may differ from the reference program's by a relative error of at most 0.00092.
Values may be sent and summed in bfloat16 or wider, within the bound.
A program may use at most 64 MiB of HBM per device.

```python
import math
import jax
import jax.numpy as jnp
from jax import lax

CELLS = 128
TRAJ = 64
BR = 16
KM = 4
KG = 1
GG = 2
STEPS = 2
K = 6
MSLOTS = 64
GSLOTS = 16
NB = 8192
DEVICES = 512


def spread_slots(key, count, slots):
    keys = jax.random.split(key, DEVICES)
    perms = jax.vmap(lambda one: jax.random.permutation(one, BR * count))(keys)
    return (perms % slots).reshape(DEVICES * BR, count).astype(jnp.int32)


def draw_member_col(key, part):
    return spread_slots(jax.random.fold_in(key, 11), KM, MSLOTS)


def draw_group_col(key, part):
    return spread_slots(jax.random.fold_in(key, 23), KG, GSLOTS)


def place_ends(values, key, low, top_value):
    spot = [jax.random.randint(jax.random.fold_in(key, axis), (), 0, length) for axis, length in enumerate(values.shape)]
    main_axis = values.shape.index(max(values.shape))
    next_to = spot[:main_axis] + [(spot[main_axis] + 1) % values.shape[main_axis]] + spot[main_axis + 1:]
    return values.at[tuple(spot)].set(low).at[tuple(next_to)].set(top_value)


def steps_of(key, extent, cuts, least, top_value):
    level = 1.0
    for axis_at, shards_of in cuts:
        heights = jax.random.uniform(jax.random.fold_in(jax.random.fold_in(key, 6), axis_at), (shards_of,), jnp.float32, least / len(cuts), top_value / len(cuts))
        level = level * jnp.repeat(jnp.exp(heights), extent[axis_at] // shards_of).reshape((-1,) + (1,) * (len(extent) - 1 - axis_at))
    return level


def centred(key, shape, deviation, limit, shards=(), kind=jnp.bfloat16):
    values = deviation * jax.random.normal(key, shape, jnp.float32)
    if shards:
        values = values * steps_of(key, shape, shards, -0.22, 0.18)
    return jnp.clip(values, -limit, limit).astype(kind)


def setup_inputs(seed: int = 0) -> dict:
    key_list = jax.random.split(jax.random.key(seed), 9)
    state = centred(key_list[0], (NB, TRAJ, CELLS), 0.6, 2.5, ((0, 512),), jnp.float32)
    blocks = centred(key_list[1], (NB, K, CELLS, CELLS), (CELLS // 4) ** -0.5, 1.0, ((0, 512),))
    rate = jnp.clip(jnp.exp(math.log(1.0) - 2.3025851 * jax.random.uniform(key_list[2], (NB, CELLS), jnp.float32) ** steps_of(key_list[2], (NB, CELLS), ((0, 512),), -0.2, 0.2)), 0.1, 1.0)
    own_col = place_ends(jax.random.randint(key_list[3], (NB,), 0, BR), jax.random.fold_in(key_list[3], 1), 0, BR - 1).astype(jnp.int32)
    member_col = draw_member_col(jax.random.fold_in(key_list[8], 71), 0)
    group_col = draw_group_col(jax.random.fold_in(key_list[8], 71), 0)
    member_send = place_ends(jax.random.randint(key_list[6], (DEVICES, MSLOTS), 0, BR), jax.random.fold_in(key_list[6], 1), 0, BR - 1).astype(jnp.int32)
    group_send = place_ends(jax.random.randint(key_list[7], (DEVICES, GSLOTS), 0, BR), jax.random.fold_in(key_list[7], 1), 0, BR - 1).astype(jnp.int32)
    return {"state": state, "blocks": blocks, "rate": rate, "own_col": own_col, "member_col": member_col, "group_col": group_col, "member_send": member_send, "group_send": group_send}


step_size = 0.1


def sources(own_col, member_col, group_col, member_send, group_send):
    rows = jnp.arange(NB, dtype=jnp.int32)
    device = rows // BR
    grp = device // MSLOTS
    mem = device % MSLOTS
    own_src = device * BR + own_col
    peer_dev = grp[:, None] * MSLOTS + member_col
    member_src = peer_dev * BR + member_send[peer_dev, mem[:, None]]
    hgroup = group_col // GG
    within = group_col % GG
    far_dev = hgroup * MSLOTS + mem[:, None]
    group_src = far_dev * BR + group_send[far_dev, grp[:, None] * GG + within]
    return jnp.concatenate([own_src[:, None], member_src, group_src], axis=1).astype(jnp.int32)


def derivative(field, blocks, rate, src):
    rounded = field.astype(jnp.bfloat16)

    def one_device(device):
        start = (device * BR).astype(jnp.int32)
        index = lax.dynamic_slice_in_dim(src, start, BR, 0)
        taken = rounded[index].astype(jnp.float32)
        weights = lax.dynamic_slice_in_dim(blocks, start, BR, 0).astype(jnp.float32)
        return jnp.einsum('iktc,ikcd->itd', taken, weights, precision=lax.Precision.HIGHEST)

    product = lax.map(one_device, jnp.arange(DEVICES, dtype=jnp.int32))
    product = product.reshape(NB, TRAJ, CELLS)
    return -product + rate[:, None, :] * (field - field * field * field)


def reference(state, blocks, rate, own_col, member_col, group_col, member_send, group_send):
    src = sources(own_col, member_col, group_col, member_send, group_send)
    current = state
    for step in range(STEPS):
        first = derivative(current, blocks, rate, src)
        second = derivative(current + 0.5 * step_size * first, blocks, rate, src)
        third = derivative(current + 0.5 * step_size * second, blocks, rate, src)
        fourth = derivative(current + step_size * third, blocks, rate, src)
        current = current + (step_size / 6.0) * (first + 2.0 * second + 2.0 * third + fourth)
    return current
```

```python
import functools

import jax
import jax.numpy as jnp
from jax import lax
from jax.experimental import pallas as pl
from jax.experimental.pallas import tpu as pltpu
from jax.sharding import PartitionSpec as P

MESH = pl.DeviceIdType.MESH
STEPS = 2
STEP_SIZE = 0.1
EVALS = 4 * STEPS

X = 4
Z = 16
DEPTH = 4
HALVES = 2


def slot_of(back):
    half, base = Z // 2, 2 * DEPTH + 1
    side = half - DEPTH - 1
    up = Z - back
    low = jnp.where(back <= DEPTH, back, base + back - DEPTH - 1)
    high = jnp.where(up <= DEPTH, DEPTH + up, base + side + up - DEPTH - 1)
    return jnp.where(back == half, Z - 1, jnp.where(back < half, low, high))


def kernel(
    groups, rows, per_group,
    table, own_col, group_send, zblk, zsum, gblk, gsum,
    state, blocks, rate,
    out,
    own, field, total, lands, local0, local1, near, far, xin, fpack, gpack, gin,
    zprod, gprod, oprod,
    z_send, z_recv, f_send, f_recv, xn_send, xn_recv, xf_send, xf_recv, g_send, g_recv,
):
    half = Z // 2
    nears = 2 * DEPTH + 1
    side = half - DEPTH - 1
    traj = own.shape[2]
    local = (local0, local1)
    g = lax.axis_index("group")
    m = lax.axis_index("member")
    x, z = m // Z, m % Z

    def at_z(step):
        return (z + step + Z) % Z

    def member(xx, zz):
        return xx * Z + zz

    def along_z(step):
        return (g, member(x, at_z(step)))

    def along_x(step):
        return (g, member((x + step) % X, z))

    partners = [along_z(s * d) for d in range(1, max(1, half - DEPTH) + 1) for s in (1, -1)]
    partners += [along_x(j) for j in range(1, X)]
    partners += [((g + o) % groups, m) for o in range(1, groups)]
    barrier = pltpu.get_barrier_semaphore()
    for partner in partners:
        pl.semaphore_signal(barrier, inc=1, device_id=partner, device_id_type=MESH)
    pl.semaphore_wait(barrier, len(partners))

    def remote(src, dst, send, recv, device):
        return pltpu.make_async_remote_copy(
            src_ref=src, dst_ref=dst, send_sem=send, recv_sem=recv,
            device_id=device, device_id_type=MESH,
        )

    def z_copy(p, h, side_, t):
        src = own.at[h] if t == 0 else lands.at[p, h, side_, t - 1]
        return remote(
            src, lands.at[p, h, side_, t], z_send.at[h, side_, t], z_recv.at[p, h, side_, t],
            along_z(1 if side_ == 0 else -1),
        )

    def f_copy(p, h, side_, d):
        if d == half - DEPTH:
            js = pl.ds(0, X // 2) if side_ == 0 else pl.ds(X // 2, X // 2)
            slot = side * 2
        else:
            js = pl.ds(0, X)
            slot = side_ * side + d - 1
        return remote(
            fpack.at[h, side_, d - 1, js], far.at[p, h, js, slot],
            f_send.at[h, side_, d - 1], f_recv.at[p, h, side_, d - 1],
            along_z(d if side_ == 0 else -d),
        )

    def xn_copy(p, h, j):
        return remote(
            near.at[h, j], xin.at[p, h, j - 1, pl.ds(0, nears)],
            xn_send.at[h, j - 1], xn_recv.at[p, h, j - 1], along_x(j),
        )

    def xf_copy(p, h, j):
        return remote(
            far.at[p, h, j], xin.at[p, h, j - 1, pl.ds(nears, Z - nears)],
            xf_send.at[h, j - 1], xf_recv.at[p, h, j - 1], along_x(j),
        )

    def g_copy(p, h, o):
        return remote(
            gpack.at[h, pl.ds(o * per_group, per_group)],
            gin.at[p, h, pl.ds((o - 1) * per_group, per_group)],
            g_send.at[h, o - 1], g_recv.at[p, h, o - 1], ((g + o) % groups, m),
        )

    def product(left, block):
        return jnp.dot(left, blocks[block], preferred_element_type=jnp.float32)

    def first(h):
        part = slice(h * traj, (h + 1) * traj)

        def row(i, _):
            value = state[i, part, :]
            out[i, part, :] = value
            field[h, i] = value
            own[h, i] = value.astype(jnp.bfloat16)
            return 0

        lax.fori_loop(0, rows, row, 0)

    def begin(e, h):
        p = e % 2
        for side_ in (0, 1):
            z_copy(p, h, side_, 0).start()
        for o in range(groups):
            target = (g + o) % groups
            for s in range(per_group):
                gpack[h, o * per_group + s] = own[h, group_send[target * per_group + s]]
        for o in range(1, groups):
            g_copy(p, h, o).start()
        for j in range(X):
            near[h, j, 0] = own[h, table[m, member((x + j) % X, z)]]

        def products(n, _):
            for i in range(8):
                i = n * 8 + i
                oprod[h, i] = product(own[h, own_col[i]], i * K_ALL)
            return 0

        lax.fori_loop(0, rows // 8, products, 0)

    def step(e, h, t):
        p = e % 2
        for side_ in (0, 1):
            z_copy(p, h, side_, t - 1).wait_recv()
            if t < DEPTH:
                z_copy(p, h, side_, t).start()
            local[side_][...] = lands[p, h, side_, t - 1]
        for side_ in (0, 1):
            back = t if side_ == 0 else -t
            source = member(x, at_z(-back))
            if t == DEPTH:
                for d in range(1, half - DEPTH + 1):
                    js = range(X)
                    if d == half - DEPTH:
                        js = js[: X // 2] if side_ == 0 else js[X // 2 :]
                    there = at_z(d if side_ == 0 else -d)
                    for j in js:
                        fpack[h, side_, d - 1, j] = local[side_][table[source, member((x + j) % X, there)]]
                    f_copy(p, h, side_, d).start()
        for side_ in (0, 1):
            back = t if side_ == 0 else -t
            source = member(x, at_z(-back))
            for j in range(X):
                near[h, j, side_ * DEPTH + t] = local[side_][table[source, member((x + j) % X, z)]]
        if t == DEPTH:
            for j in range(1, X):
                xn_copy(p, h, j).start()

    def group_products(e, h):
        p = e % 2
        for o in range(1, groups):
            g_copy(p, h, o).wait_recv()
        for s in range(per_group):
            gprod[h, s] = product(gpack[h, s], gblk[s])

        def products(n, _):
            for s in range(per_group):
                k = n * per_group + s
                gprod[h, k + per_group] = product(gin[p, h, k], gblk[k + per_group])
            return 0

        lax.fori_loop(0, groups - 1, products, 0)

    def across(e, h):
        p = e % 2
        for side_ in (0, 1):
            for d in range(1, half - DEPTH + 1):
                f_copy(p, h, side_, d).wait_recv()
        for j in range(1, X):
            xf_copy(p, h, j).start()
        for s in range(nears):
            zprod[h, s] = product(near[h, 0, s], zblk[s])
        for s in range(nears, Z):
            zprod[h, s] = product(far[p, h, 0, s - nears], zblk[s])
        for j in range(1, X):
            xn_copy(p, h, j).wait_recv()

        def products(j, _):
            for s in range(nears):
                zprod[h, (j + 1) * Z + s] = product(xin[p, h, j, s], zblk[(j + 1) * Z + s])
            return 0

        lax.fori_loop(0, X - 1, products, 0)

    def finish(e, h):
        p = e % 2
        for j in range(1, X):
            xf_copy(p, h, j).wait_recv()

        def products(j, _):
            for s in range(nears, Z):
                zprod[h, (j + 1) * Z + s] = product(xin[p, h, j, s], zblk[(j + 1) * Z + s])
            return 0

        lax.fori_loop(0, X - 1, products, 0)
        for side_ in (0, 1):
            for t in range(DEPTH):
                z_copy(p, h, side_, t).wait_send()
            for d in range(1, half - DEPTH + 1):
                f_copy(p, h, side_, d).wait_send()
        for j in range(1, X):
            xn_copy(p, h, j).wait_send()
            xf_copy(p, h, j).wait_send()
        for o in range(1, groups):
            g_copy(p, h, o).wait_send()

        part = slice(h * traj, (h + 1) * traj)
        stage = e % 4
        is_first, is_last = stage == 0, stage == 3
        weight = jnp.where(is_first | is_last, 1.0, 2.0).astype(jnp.float32)
        ahead = jnp.where(stage == 2, STEP_SIZE, 0.5 * STEP_SIZE).astype(jnp.float32)
        members = zsum.shape[0] // rows

        def update(i):
            y = oprod[h, i] + gprod[h, gsum[i]]
            for k in range(members):
                y = y + zprod[h, zsum[i * members + k]]
            v = field[h, i]
            u = out[i, part, :]
            slope = rate[pl.ds(i, 1), :] * (v - v * v * v) - y
            before = jnp.where(is_first, 0.0, total[h, i])
            summed = before + weight * slope
            total[h, i] = summed
            value = u + jnp.where(is_last, (STEP_SIZE / 6.0) * summed, ahead * slope)
            out[i, part, :] = jnp.where(is_last, value, u)
            field[h, i] = value
            own[h, i] = value.astype(jnp.bfloat16)

        def four(n, _):
            for i in range(4):
                update(n * 4 + i)
            return 0

        lax.fori_loop(0, rows // 4, four, 0)

    K_ALL = blocks.shape[0] // rows

    first(0)
    first(1)

    def stages(h):
        parts = [lambda e: begin(e, h)]
        for t in range(1, DEPTH + 1):
            parts.append(lambda e, t=t: step(e, h, t))
        parts.append(lambda e: across(e, h))
        return parts

    a, b = stages(0), stages(1)
    cut = (len(a) + 1) // 2

    def evaluation(i, _):
        after = i >= 1
        ahead = i < EVALS

        def late(fn):
            pl.when(after)(lambda: fn(i - 1))

        def now(fn):
            pl.when(ahead)(lambda: fn(i))

        late(lambda e: finish(e, 0))
        for n in range(cut):
            now(a[n])
            if n == 1:
                now(lambda e: group_products(e, 0))
            if cut + n < len(b):
                late(b[cut + n])
        late(lambda e: finish(e, 1))
        for n in range(cut):
            now(b[n])
            if n == 1:
                now(lambda e: group_products(e, 1))
            if cut + n < len(a):
                now(a[cut + n])
        return 0

    lax.fori_loop(0, EVALS + 1, evaluation, 0)


def per_device(groups, state, blocks, rate, own_col, member_col, group_col, member_send, group_send):
    rows, traj, cells = state.shape
    members = member_col.shape[1]
    count = blocks.shape[1]
    per_group = group_send.shape[1] // groups
    part = traj // HALVES
    half, nears = Z // 2, 2 * DEPTH + 1
    g = lax.axis_index("group")
    m = lax.axis_index("member")
    x, z = m // Z, m % Z

    table = lax.all_gather(member_send[0], "member", axis=0)
    col = member_col.reshape(-1)
    zsum = ((x - col // Z + X) % X) * Z + slot_of((z - col % Z + Z) % Z)
    ids = jnp.arange(rows * members, dtype=jnp.int32)
    block_of = (ids // members) * count + 1 + ids % members
    zblk = jnp.sum(jnp.where(zsum[None, :] == ids[:, None], block_of[None, :], 0), axis=1)
    gcol = group_col.reshape(-1)
    gsum = ((g - gcol // per_group + groups) % groups) * per_group + gcol % per_group
    gids = jnp.arange(gcol.shape[0], dtype=jnp.int32)
    gblock = gids * count + count - 1
    gblk = jnp.sum(jnp.where(gsum[None, :] == gids[:, None], gblock[None, :], 0), axis=1)

    smem = pl.BlockSpec(memory_space=pltpu.SMEM)
    vmem = pl.BlockSpec(memory_space=pltpu.VMEM)
    bf, f32 = jnp.bfloat16, jnp.float32
    tile = (part, cells)
    dma = pltpu.SemaphoreType.DMA
    return pl.pallas_call(
        functools.partial(kernel, groups, rows, per_group),
        out_shape=jax.ShapeDtypeStruct(state.shape, f32),
        in_specs=[smem] * 7 + [vmem] * 3,
        out_specs=vmem,
        scratch_shapes=[
            pltpu.VMEM((HALVES, rows) + tile, bf),
            pltpu.VMEM((HALVES, rows) + tile, f32),
            pltpu.VMEM((HALVES, rows) + tile, f32),
            pltpu.VMEM((2, HALVES, 2, DEPTH, rows) + tile, bf),
            pltpu.VMEM((rows,) + tile, bf),
            pltpu.VMEM((rows,) + tile, bf),
            pltpu.VMEM((HALVES, X, nears) + tile, bf),
            pltpu.VMEM((2, HALVES, X, Z - nears) + tile, bf),
            pltpu.VMEM((2, HALVES, X - 1, Z) + tile, bf),
            pltpu.VMEM((HALVES, 2, half - DEPTH, X) + tile, bf),
            pltpu.VMEM((HALVES, groups * per_group) + tile, bf),
            pltpu.VMEM((2, HALVES, (groups - 1) * per_group) + tile, bf),
            pltpu.VMEM((HALVES, X * Z) + tile, f32),
            pltpu.VMEM((HALVES, groups * per_group) + tile, f32),
            pltpu.VMEM((HALVES, rows) + tile, f32),
            dma((HALVES, 2, DEPTH)),
            dma((2, HALVES, 2, DEPTH)),
            dma((HALVES, 2, half - DEPTH)),
            dma((2, HALVES, 2, half - DEPTH)),
            dma((HALVES, X - 1)),
            dma((2, HALVES, X - 1)),
            dma((HALVES, X - 1)),
            dma((2, HALVES, X - 1)),
            dma((HALVES, groups - 1)),
            dma((2, HALVES, groups - 1)),
        ],
        compiler_params=pltpu.CompilerParams(
            collective_id=0, has_side_effects=True, vmem_limit_bytes=48 * 2**20
        ),
        cost_estimate=pl.CostEstimate(
            flops=EVALS * 2 * rows * count * traj * cells * cells,
            bytes_accessed=4 * 2**20, transcendentals=0,
        ),
    )(
        table, own_col, group_send[0], zblk.astype(jnp.int32), zsum.astype(jnp.int32),
        gblk.astype(jnp.int32), gsum.astype(jnp.int32),
        state, blocks.reshape(rows * count, cells, cells), rate,
    )


def solution(mesh):
    return jax.shard_map(
        functools.partial(per_device, mesh.shape["group"]),
        mesh=mesh,
        in_specs=(
            P(("group", "member"), None, None),
            P(("group", "member"), None, None, None),
            P(("group", "member"), None),
            P(("group", "member")),
            P(("group", "member"), None),
            P(("group", "member"), None),
            P(("group", "member"), None),
            P(("group", "member"), None),
        ),
        out_specs=P(("group", "member"), None, None),
        check_vma=False,
    )
```

```python
import functools

import jax
import jax.numpy as jnp
from jax import lax
from jax.experimental import pallas as pl
from jax.experimental.pallas import tpu as pltpu
from jax.sharding import PartitionSpec as P

MESH = pl.DeviceIdType.MESH
STEPS = 2
STEP_SIZE = 0.1
EVALS = 4 * STEPS

X = 4
Z = 16
DEPTH = 3
PARTS = 4
ORDER = (("turn", 0), ("3", 2), ("across", 3), ("2", 1), ("1", 0), ("group", 0))


def slot_of(back):
    half, base = Z // 2, 2 * DEPTH + 1
    side = half - DEPTH - 1
    up = Z - back
    low = jnp.where(back <= DEPTH, back, base + back - DEPTH - 1)
    high = jnp.where(up <= DEPTH, DEPTH + up, base + side + up - DEPTH - 1)
    return jnp.where(back == half, Z - 1, jnp.where(back < half, low, high))


def kernel(
    groups, rows, per_group,
    numbers, own_table, state, blocks_in, rate,
    out,
    blocks, table_in, table, table_send, table_recv, load_sem,
    own, field, total, lands, local0, local1, near, far, xin, fpack, gpack, gin,
    zprod, gprod, oprod,
    z_send, z_recv, f_send, f_recv, xn_send, xn_recv, xf_send, xf_recv, g_send, g_recv,
):
    half = Z // 2
    nears = 2 * DEPTH + 1
    count = blocks.shape[0] // rows
    side = half - DEPTH - 1
    traj = own.shape[2]
    local = (local0, local1)
    g = lax.axis_index("group")
    m = lax.axis_index("member")
    x, z = m // Z, m % Z

    def at_z(step):
        return (z + step + Z) % Z

    def member(xx, zz):
        return xx * Z + zz

    def along_z(step):
        return (g, member(x, at_z(step)))

    def along_x(step):
        return (g, member((x + step) % X, z))

    reach = max(DEPTH, half - DEPTH)
    partners = [along_z(s * d) for d in range(1, reach + 1) for s in (1, -1)]
    partners += [along_x(j) for j in range(1, X)]
    partners += [((g + o) % groups, m) for o in range(1, groups)]
    load = pltpu.make_async_copy(blocks_in, blocks, load_sem.at[0])
    load.start()
    barrier = pltpu.get_barrier_semaphore()
    for partner in partners:
        pl.semaphore_signal(barrier, inc=1, device_id=partner, device_id_type=MESH)
    pl.semaphore_wait(barrier, len(partners))

    def remote(src, dst, send, recv, device):
        return pltpu.make_async_remote_copy(
            src_ref=src, dst_ref=dst, send_sem=send, recv_sem=recv,
            device_id=device, device_id_type=MESH,
        )

    def table_copy(side_, t):
        slot = side_ * DEPTH + t - 1
        return remote(
            own_table, table_in.at[slot], table_send.at[slot], table_recv.at[slot],
            along_z(t if side_ == 0 else -t),
        )

    members = X * Z // rows
    zblk_at = 0
    zsum_at = zblk_at + X * Z
    gblk_at = zsum_at + X * Z
    gsum_at = gblk_at + groups * per_group
    own_at = gsum_at + rows
    gsend_at = own_at + rows
    send_at = gsend_at + groups * per_group

    def picked(side_, t, to):
        return table[side_ * DEPTH + t - 1, 0, to]

    def z_copy(p, h, side_, t):
        src = own.at[h] if t == 0 else lands.at[p, h, side_, t - 1]
        return remote(
            src, lands.at[p, h, side_, t], z_send.at[h, side_, t], z_recv.at[p, h, side_, t],
            along_z(1 if side_ == 0 else -1),
        )

    def f_copy(p, h, side_, d):
        if d == half - DEPTH:
            js = pl.ds(0, X // 2) if side_ == 0 else pl.ds(X // 2, X // 2)
            slot = side * 2
        else:
            js = pl.ds(0, X)
            slot = side_ * side + d - 1
        return remote(
            fpack.at[h, side_, d - 1, js], far.at[p, h, js, slot],
            f_send.at[h, side_, d - 1], f_recv.at[p, h, side_, d - 1],
            along_z(d if side_ == 0 else -d),
        )

    def xn_copy(p, h, j):
        return remote(
            near.at[h, j], xin.at[p, h, j - 1, pl.ds(0, nears)],
            xn_send.at[h, j - 1], xn_recv.at[p, h, j - 1], along_x(j),
        )

    def xf_copy(p, h, j):
        return remote(
            far.at[p, h, j], xin.at[p, h, j - 1, pl.ds(nears, Z - nears)],
            xf_send.at[h, j - 1], xf_recv.at[p, h, j - 1], along_x(j),
        )

    def g_copy(p, h, o):
        return remote(
            gpack.at[h, pl.ds(o * per_group, per_group)],
            gin.at[p, h, pl.ds((o - 1) * per_group, per_group)],
            g_send.at[h, o - 1], g_recv.at[p, h, o - 1], ((g + o) % groups, m),
        )

    def product(left, block):
        return jnp.dot(left, blocks[block], preferred_element_type=jnp.float32)

    def part_of(h):
        return pl.ds(pl.multiple_of(h * traj, traj), traj)

    def first(h):
        part = part_of(h)

        def row(i, _):
            value = state[i, part, :]
            out[i, part, :] = value
            field[h, i] = value
            own[h, i] = value.astype(jnp.bfloat16)
            return 0

        lax.fori_loop(0, rows, row, 0)

    def launch(e, h):
        for side_ in (0, 1):
            z_copy(e % 2, h, side_, 0).start()

    def begin(e, h):
        p = e % 2
        for o in range(groups):
            target = (g + o) % groups
            for s in range(per_group):
                gpack[h, o * per_group + s] = own[h, numbers[gsend_at + target * per_group + s]]
        for o in range(1, groups):
            g_copy(p, h, o).start()
        for j in range(X):
            near[h, j, 0] = own[h, numbers[send_at + member((x + j) % X, z)]]

        def products(n, _):
            for i in range(8):
                i = n * 8 + i
                oprod[h, i] = product(own[h, numbers[own_at + i]], i * count)
            return 0

        lax.fori_loop(0, rows // 8, products, 0)

    def step(e, h, t):
        p = e % 2
        for side_ in (0, 1):
            z_copy(p, h, side_, t - 1).wait_recv()
            if t < DEPTH:
                z_copy(p, h, side_, t).start()
            local[side_][...] = lands[p, h, side_, t - 1]
        for side_ in (0, 1):
            if t == DEPTH:
                for d in range(1, half - DEPTH + 1):
                    js = range(X)
                    if d == half - DEPTH:
                        js = js[: X // 2] if side_ == 0 else js[X // 2 :]
                    there = at_z(d if side_ == 0 else -d)
                    for j in js:
                        fpack[h, side_, d - 1, j] = local[side_][picked(side_, t, member((x + j) % X, there))]
                    f_copy(p, h, side_, d).start()
        for side_ in (0, 1):
            for j in range(X):
                near[h, j, side_ * DEPTH + t] = local[side_][picked(side_, t, member((x + j) % X, z))]
        if t == DEPTH:
            for j in range(1, X):
                xn_copy(p, h, j).start()

    def group_products(e, h):
        p = e % 2
        for o in range(1, groups):
            g_copy(p, h, o).wait_recv()
        for s in range(per_group):
            gprod[h, s] = product(gpack[h, s], numbers[gblk_at + s])

        def products(n, _):
            for s in range(per_group):
                k = n * per_group + s
                gprod[h, k + per_group] = product(gin[p, h, k], numbers[gblk_at + k + per_group])
            return 0

        lax.fori_loop(0, groups - 1, products, 0)

    def across(e, h):
        p = e % 2
        for side_ in (0, 1):
            for d in range(1, half - DEPTH + 1):
                f_copy(p, h, side_, d).wait_recv()
        for j in range(1, X):
            xf_copy(p, h, j).start()
        for s in range(nears):
            zprod[h, s] = product(near[h, 0, s], numbers[zblk_at + s])
        for s in range(nears, Z):
            zprod[h, s] = product(far[p, h, 0, s - nears], numbers[zblk_at + s])
        for j in range(1, X):
            xn_copy(p, h, j).wait_recv()

        def products(j, _):
            for s in range(nears):
                zprod[h, (j + 1) * Z + s] = product(xin[p, h, j, s], numbers[zblk_at + (j + 1) * Z + s])
            return 0

        lax.fori_loop(0, X - 1, products, 0)

    def finish(e, h):
        p = e % 2
        for j in range(1, X):
            xf_copy(p, h, j).wait_recv()

        def products(j, _):
            for s in range(nears, Z):
                zprod[h, (j + 1) * Z + s] = product(xin[p, h, j, s], numbers[zblk_at + (j + 1) * Z + s])
            return 0

        lax.fori_loop(0, X - 1, products, 0)
        for side_ in (0, 1):
            for t in range(DEPTH):
                z_copy(p, h, side_, t).wait_send()
            for d in range(1, half - DEPTH + 1):
                f_copy(p, h, side_, d).wait_send()
        for j in range(1, X):
            xn_copy(p, h, j).wait_send()
            xf_copy(p, h, j).wait_send()
        for o in range(1, groups):
            g_copy(p, h, o).wait_send()

        part = part_of(h)
        stage = e % 4
        is_first, is_last = stage == 0, stage == 3
        weight = jnp.where(is_first | is_last, 1.0, 2.0).astype(jnp.float32)
        ahead = jnp.where(stage == 2, STEP_SIZE, 0.5 * STEP_SIZE).astype(jnp.float32)

        def update(i):
            y = oprod[h, i] + gprod[h, numbers[gsum_at + i]]
            for k in range(members):
                y = y + zprod[h, numbers[zsum_at + i * members + k]]
            v = field[h, i]
            u = out[i, part, :]
            slope = rate[pl.ds(i, 1), :] * (v - v * v * v) - y
            before = jnp.where(is_first, 0.0, total[h, i])
            summed = before + weight * slope
            total[h, i] = summed
            value = u + jnp.where(is_last, (STEP_SIZE / 6.0) * summed, ahead * slope)
            out[i, part, :] = jnp.where(is_last, value, u)
            field[h, i] = value
            own[h, i] = value.astype(jnp.bfloat16)

        def four(n, _):
            for i in range(4):
                update(n * 4 + i)
            return 0

        lax.fori_loop(0, rows // 4, four, 0)
        pl.when(e + 1 < EVALS)(lambda: launch(e + 1, h))

    copies = [table_copy(side_, t) for t in range(1, DEPTH + 1) for side_ in (0, 1)]
    for copy in copies:
        copy.start()

    def open_part(h, _):
        first(h)
        launch(0, h)
        return 0

    lax.fori_loop(0, PARTS, open_part, 0)
    for copy in copies:
        copy.wait_recv()
    fetch = pltpu.make_async_copy(table_in, table, load_sem.at[1])
    fetch.start()
    fetch.wait()
    for copy in copies:
        copy.wait_send()
    load.wait()

    turns = PARTS * EVALS

    def turn(n, _):
        def at(lag, last, what):
            k = n - lag

            def run():
                what(lax.div(k, PARTS), lax.rem(k, PARTS))

            pl.when((k >= 0) & (k < last))(run)

        for name, lag in ORDER:
            if name == "turn":
                pl.when(n >= PARTS)(lambda: finish(lax.div(n, PARTS) - 1, lax.rem(n, PARTS)))
                at(0, turns, begin)
            elif name == "across":
                at(lag, turns, across)
            elif name == "group":
                at(lag, turns, group_products)
            else:
                at(lag, turns, lambda e, h, t=int(name): step(e, h, t))
        return 0

    lax.fori_loop(0, turns + PARTS, turn, 0)


def per_device(groups, state, blocks, rate, own_col, member_col, group_col, member_send, group_send):
    rows, traj, cells = state.shape
    members = member_col.shape[1]
    count = blocks.shape[1]
    per_group = group_send.shape[1] // groups
    part = traj // PARTS
    half, nears = Z // 2, 2 * DEPTH + 1
    g = lax.axis_index("group")
    m = lax.axis_index("member")
    x, z = m // Z, m % Z

    col = member_col.reshape(-1)
    zsum = ((x - col // Z + X) % X) * Z + slot_of((z - col % Z + Z) % Z)
    ids = jnp.arange(rows * members, dtype=jnp.int32)
    block_of = (ids // members) * count + 1 + ids % members
    zblk = jnp.sum(jnp.where(zsum[None, :] == ids[:, None], block_of[None, :], 0), axis=1)
    gcol = group_col.reshape(-1)
    gsum = ((g - gcol // per_group + groups) % groups) * per_group + gcol % per_group
    gids = jnp.arange(gcol.shape[0], dtype=jnp.int32)
    gblock = gids * count + count - 1
    gblk = jnp.sum(jnp.where(gsum[None, :] == gids[:, None], gblock[None, :], 0), axis=1)

    numbers = jnp.concatenate(
        [zblk, zsum, gblk, gsum, own_col, group_send[0], member_send[0]]
    ).astype(jnp.int32)
    own_table = jnp.pad(member_send, ((0, 0), (0, -member_send.shape[1] % cells)))

    smem = pl.BlockSpec(memory_space=pltpu.SMEM)
    vmem = pl.BlockSpec(memory_space=pltpu.VMEM)
    bf, f32 = jnp.bfloat16, jnp.float32
    tile = (part, cells)
    dma = pltpu.SemaphoreType.DMA
    return pl.pallas_call(
        functools.partial(kernel, groups, rows, per_group),
        out_shape=jax.ShapeDtypeStruct(state.shape, f32),
        in_specs=[smem, vmem, vmem, pl.BlockSpec(memory_space=pl.ANY), vmem],
        out_specs=vmem,
        scratch_shapes=[
            pltpu.VMEM((rows * count, cells, cells), bf),
            pltpu.VMEM((2 * DEPTH,) + own_table.shape, jnp.int32),
            pltpu.SMEM((2 * DEPTH,) + own_table.shape, jnp.int32),
            dma((2 * DEPTH,)),
            dma((2 * DEPTH,)),
            dma((2,)),
            pltpu.VMEM((PARTS, rows) + tile, bf),
            pltpu.VMEM((PARTS, rows) + tile, f32),
            pltpu.VMEM((PARTS, rows) + tile, f32),
            pltpu.VMEM((2, PARTS, 2, DEPTH, rows) + tile, bf),
            pltpu.VMEM((rows,) + tile, bf),
            pltpu.VMEM((rows,) + tile, bf),
            pltpu.VMEM((PARTS, X, nears) + tile, bf),
            pltpu.VMEM((2, PARTS, X, Z - nears) + tile, bf),
            pltpu.VMEM((2, PARTS, X - 1, Z) + tile, bf),
            pltpu.VMEM((PARTS, 2, half - DEPTH, X) + tile, bf),
            pltpu.VMEM((PARTS, groups * per_group) + tile, bf),
            pltpu.VMEM((2, PARTS, (groups - 1) * per_group) + tile, bf),
            pltpu.VMEM((PARTS, X * Z) + tile, f32),
            pltpu.VMEM((PARTS, groups * per_group) + tile, f32),
            pltpu.VMEM((PARTS, rows) + tile, f32),
            dma((PARTS, 2, DEPTH)),
            dma((2, PARTS, 2, DEPTH)),
            dma((PARTS, 2, half - DEPTH)),
            dma((2, PARTS, 2, half - DEPTH)),
            dma((PARTS, X - 1)),
            dma((2, PARTS, X - 1)),
            dma((PARTS, X - 1)),
            dma((2, PARTS, X - 1)),
            dma((PARTS, groups - 1)),
            dma((2, PARTS, groups - 1)),
        ],
        compiler_params=pltpu.CompilerParams(
            collective_id=0, has_side_effects=True, vmem_limit_bytes=60 * 2**20
        ),
        cost_estimate=pl.CostEstimate(
            flops=EVALS * 2 * rows * count * traj * cells * cells,
            bytes_accessed=4 * 2**20, transcendentals=0,
        ),
    )(
        numbers, own_table, state, blocks.reshape(rows * count, cells, cells), rate,
    )


def solution(mesh):
    return jax.shard_map(
        functools.partial(per_device, mesh.shape["group"]),
        mesh=mesh,
        in_specs=(
            P(("group", "member"), None, None),
            P(("group", "member"), None, None, None),
            P(("group", "member"), None),
            P(("group", "member")),
            P(("group", "member"), None),
            P(("group", "member"), None),
            P(("group", "member"), None),
            P(("group", "member"), None),
        ),
        out_specs=P(("group", "member"), None, None),
        check_vma=False,
    )
```
